256 devices in a mesh: chain: 32 (over z, x), sector: 8 (over y, core).
Axes of the slice: x: 4, y: 4, z: 8, core: 2. Of those that a mesh axis runs over, the one named last changes fastest.
Arguments:
- left_env: bfloat16 [32, 8, 14, 256, 256], P('chain', 'sector'), may hold values from -6 to 6
- right_env: bfloat16 [32, 8, 14, 256, 256], P('chain', 'sector'), may hold values from -6 to 6
- left_state: bfloat16 [32, 8, 4, 256, 256], P('chain', 'sector'), may hold values from -0.375 to 0.375
- right_state: bfloat16 [32, 8, 4, 256, 256], P('chain', 'sector'), may hold values from -0.375 to 0.375
- mpo: bfloat16 [14, 4, 4, 14], replicated, may hold values from -1.5 to 1.5
- couple: int32 [32, 4, 8], P('chain', None, 'sector'), may hold values 0 or 1
- sizes: int32 [8], replicated, may hold values from 1 to 256, 1536 in all
Outputs:
- left_out: bfloat16 [32, 8, 14, 256, 256], P('chain', 'sector')
- right_out: bfloat16 [32, 8, 14, 256, 256], P('chain', 'sector')
The draws below stay inside these ranges and needn't reach their ends.
Inputs may be any that keep to these rules, and one draw needn't show every extreme that they name: The 8 sizes sum to 1536.
All inputs are finite; a program needn't handle non-finite values. No bound on the sum of `couple` on one device may be relied on, other than what follows from the above.
Results may differ from the reference program's by a relative error of at most 0.0057.
Values may be sent and summed in bfloat16 or wider, within the bound.
A program may use at most 128 MiB of HBM per device.

```python
import math
import jax
import jax.numpy as jnp
import numpy as np
from jax import lax

M = 256
W = 14
PHYS = 4
NB = 8
SITES = 32
BOND = 1536


def touch_ends(drawn, own_key, smallest, largest):
    longest = drawn.shape.index(max(drawn.shape))
    spots = []
    for shift in (0, 1):
        where = [jax.random.randint(jax.random.fold_in(own_key, axis), (), 0, length) for axis, length in enumerate(drawn.shape)]
        where[longest] = (where[longest] + shift) % drawn.shape[longest]
        spots.append(tuple(where))
    return drawn.at[spots[0]].set(smallest).at[spots[1]].set(largest)


def block_levels(key, dims, pieces, low, top_value):
    gain, own = 1.0, jax.random.fold_in(key, 6)
    for axis_at, blocks in pieces:
        heights = jnp.exp(jax.random.uniform(jax.random.fold_in(own, axis_at), (blocks,), jnp.float32, low / len(pieces), top_value / len(pieces)))
        gain = gain * jnp.repeat(heights, dims[axis_at] // blocks).reshape([-1 if axis == axis_at else 1 for axis in range(len(dims))])
    return gain


def split_up(amount, total, most, lean):
    loads = [(1 << 20) // math.isqrt(rank ** lean) + 1 for rank in range(2, amount + 1)]
    rest, given = total - most - (amount - 1), [1] * (amount - 1)
    while rest > 0:
        free = [i for i in range(amount - 1) if given[i] < most]
        pool, remaining = sum([loads[i] for i in free]), rest
        for i in free:
            more = min(most - given[i], max(1, remaining * loads[i] // pool), rest)
            given[i] = given[i] + more
            rest = rest - more
    return np.array([most] + given)


def ragged(stream_key, count, total, limit, lean):
    if count == 2:
        one = jax.random.randint(stream_key, (), max(1, total - limit), min(limit, total - 1) + 1)
        return jnp.stack([one, total - one])
    sizes = jnp.asarray(split_up(count, total, limit, lean), jnp.int32)
    twos = (count - 1) // 2
    donor, sink = sizes[1:1 + 2 * twos:2], sizes[2:2 + 2 * twos:2]
    margin = jnp.minimum(donor - 1, limit - sink)
    shifted = jax.random.randint(jax.random.fold_in(stream_key, 1), (twos,), 0, 1 << 20) % (margin + 1)
    sizes = sizes.at[1:1 + 2 * twos:2].set(donor - shifted).at[2:2 + 2 * twos:2].set(sink + shifted)
    return sizes[jax.random.permutation(jax.random.fold_in(stream_key, 2), count)]


def normal_values(key, dims, deviation, bound, shards=(), kind=jnp.bfloat16):
    result = deviation * jax.random.normal(key, dims, jnp.float32)
    if shards:
        result = result * block_levels(key, dims, shards, -0.22, 0.18)
    return jnp.clip(result, -bound, bound).astype(kind)


def setup_inputs(seed: int = 0) -> dict:
    streams_of = jax.random.split(jax.random.key(seed), 8)
    left_env = normal_values(streams_of[0], (SITES, NB, W, M, M), 1.0, 6.0, ((0, 32), (1, 8)))
    right_env = normal_values(streams_of[1], (SITES, NB, W, M, M), 1.0, 6.0, ((0, 32), (1, 8)))
    left_state = normal_values(streams_of[2], (SITES, NB, PHYS, M, M), M ** -0.5, 0.375, ((0, 32), (1, 8)))
    right_state = normal_values(streams_of[3], (SITES, NB, PHYS, M, M), M ** -0.5, 0.375, ((0, 32), (1, 8)))
    mpo = normal_values(streams_of[4], (W, PHYS, PHYS, W), W ** -0.5, 1.5)
    couple = touch_ends((jax.random.randint(streams_of[5], (SITES, PHYS, NB), 0, 4) < 3).astype(jnp.int32), jax.random.fold_in(streams_of[5], 1), 0, 1)
    sizes = ragged(streams_of[6], NB, BOND, M, 1).astype(jnp.int32)
    return {"left_env": left_env, "right_env": right_env, "left_state": left_state, "right_state": right_state, "mpo": mpo, "couple": couple, "sizes": sizes}


OFFSETS = (0, 1, 1, 2)
GROUPS = ((0,), (1, 2), (3,))


def masked_site(site_tensor, couple_col, sizes, sector_pos):
    slot_size = site_tensor.shape[1]
    row_ids = jnp.arange(slot_size, dtype=jnp.int32)
    columns_live = sizes[sector_pos]
    pieces_list = []
    for physical in range(4):
        source_pos = sector_pos - OFFSETS[physical]
        live_rows = jnp.where(source_pos >= 0, sizes[jnp.maximum(source_pos, 0)], 0)
        keep_mask = (row_ids[:, None] < live_rows) & (row_ids[None, :] < columns_live) & (couple_col[physical] > 0)
        pieces_list.append(jnp.where(keep_mask, site_tensor[physical], jnp.zeros_like(site_tensor[physical])))
    return jnp.stack(pieces_list)


def left_mixer(weights, members):
    picked = weights[:, list(members)][:, :, list(members)]
    group_size = len(members)
    mpo_width = weights.shape[0]
    return jnp.transpose(picked, (1, 3, 2, 0)).reshape(group_size * mpo_width, group_size * mpo_width)


def right_mixer(weights, members):
    picked = weights[:, list(members)][:, :, list(members)]
    group_size = len(members)
    mpo_width = weights.shape[0]
    return jnp.transpose(picked, (1, 0, 2, 3)).reshape(group_size * mpo_width, group_size * mpo_width)


def left_group(env_src, site_m, weights, members):
    mpo_width, slot_size = env_src.shape[0], env_src.shape[1]
    env_wide = env_src.astype(jnp.float32)
    products = jnp.stack([jnp.einsum('wxa,ab->wxb', env_wide, site_m[physical].astype(jnp.float32)).astype(jnp.bfloat16) for physical in members])
    group_size = len(members)
    mixed_terms = jnp.dot(left_mixer(weights, members), products.reshape(group_size * mpo_width, slot_size * slot_size), preferred_element_type=jnp.float32)
    mixed_terms = mixed_terms.astype(jnp.bfloat16).reshape(group_size, mpo_width, slot_size, slot_size)
    chosen = site_m[members[0]:members[-1] + 1].astype(jnp.float32)
    return jnp.einsum('sab,svac->vbc', chosen, mixed_terms.astype(jnp.float32))


def right_group(env_blk, site_m, weights, members):
    mpo_width, slot_size = env_blk.shape[0], env_blk.shape[1]
    env_wide = env_blk.astype(jnp.float32)
    products = jnp.stack([jnp.einsum('vbc,ac->vba', env_wide, site_m[physical].astype(jnp.float32)).astype(jnp.bfloat16) for physical in members])
    group_size = len(members)
    mixed_terms = jnp.dot(right_mixer(weights, members), products.reshape(group_size * mpo_width, slot_size * slot_size), preferred_element_type=jnp.float32)
    mixed_terms = mixed_terms.astype(jnp.bfloat16).reshape(group_size, mpo_width, slot_size, slot_size)
    chosen = site_m[members[0]:members[-1] + 1].astype(jnp.float32)
    return jnp.einsum('sab,swbc->wac', chosen, mixed_terms.astype(jnp.float32))


def left_site(env_site, site_all, weights, couple_site, sizes):
    block_count = env_site.shape[0]
    padded = jnp.concatenate([jnp.zeros((2,) + env_site.shape[1:], env_site.dtype), env_site], axis=0)

    def per_block(sector_pos):
        site_m = masked_site(lax.dynamic_index_in_dim(site_all, sector_pos, 0, keepdims=False), lax.dynamic_index_in_dim(couple_site, sector_pos, 1, keepdims=False), sizes, sector_pos)
        summed = jnp.zeros(env_site.shape[1:], jnp.float32)
        for members in GROUPS:
            source_env = lax.dynamic_index_in_dim(padded, sector_pos + 2 - OFFSETS[members[0]], 0, keepdims=False)
            summed = summed + left_group(source_env, site_m, weights, members)
        return summed.astype(jnp.bfloat16)

    return lax.map(per_block, jnp.arange(block_count, dtype=jnp.int32))


def right_site(env_site, site_all, weights, couple_site, sizes):
    block_count = env_site.shape[0]

    def per_block(sector_pos):
        site_m = masked_site(lax.dynamic_index_in_dim(site_all, sector_pos, 0, keepdims=False), lax.dynamic_index_in_dim(couple_site, sector_pos, 1, keepdims=False), sizes, sector_pos)
        env_blk = lax.dynamic_index_in_dim(env_site, sector_pos, 0, keepdims=False)
        return jnp.stack([right_group(env_blk, site_m, weights, members) for members in GROUPS])

    partials = lax.map(per_block, jnp.arange(block_count, dtype=jnp.int32))
    padded = jnp.concatenate([partials, jnp.zeros((2,) + partials.shape[1:], jnp.float32)], axis=0)
    summed = partials[:, 0] + padded[1:block_count + 1, 1] + padded[2:block_count + 2, 2]
    return summed.astype(jnp.bfloat16)


def reference(left_env, right_env, left_state, right_state, mpo, couple, sizes):
    new_left = lax.map(lambda operands: left_site(operands[0], operands[1], mpo, operands[2], sizes), (left_env[:-1], left_state[:-1], couple[:-1]))
    new_right = lax.map(lambda operands: right_site(operands[0], operands[1], mpo, operands[2], sizes), (right_env[1:], right_state[1:], couple[1:]))
    left_out = jnp.concatenate([left_env[:1], new_left], axis=0)
    right_out = jnp.concatenate([new_right, right_env[-1:]], axis=0)
    return left_out, right_out
```

```python
import jax
import jax.numpy as jnp
from jax import lax
from jax.experimental import pallas as pl
from jax.experimental.pallas import tpu as pltpu
from jax.sharding import PartitionSpec as P

MESH = pl.DeviceIdType.MESH
BF = jnp.bfloat16
F32 = jnp.float32
OFFSETS = (0, 1, 1, 2)
STEP_ROWS = 32
UNIT_ROWS = 64
TILE = 16


def transposed_dot(a, b):
    return lax.dot_general(a, b, (((1,), (1,)), ((), ())), preferred_element_type=F32)


def kernel(
    chains, sectors,
    lenv, renv, lstate, rstate, mixers, couple, sizes,
    lout, rout,
    env, own, site, turned, mix0, mix3, mix12, inner, mixed, total, result,
    load_sem, x_send, x_recv, y_send, y_recv, d_send, d_recv, s_send, s_recv, out_sem,
):
    width, slot = lenv.shape[0], lenv.shape[1]
    steps, quarters = slot // STEP_ROWS, slot // UNIT_ROWS
    i = lax.axis_index("chain")
    k = lax.axis_index("sector")
    core = lax.rem(k, 2)

    def at(chain_step, sector_step):
        return (
            lax.rem(i + chain_step + chains, chains),
            lax.rem(k + sector_step + sectors, sectors),
        )

    partner = (i, k + 1 - 2 * core)
    ahead, behind = at(1, 0), at(-1, 0)
    barrier = pltpu.get_barrier_semaphore()
    greeted = (
        ahead, behind, at(0, 2), at(0, -2), partner,
        at(-1, -1), at(-1, -2), at(1, 1), at(1, 2),
    )
    for device in greeted:
        pl.semaphore_signal(barrier, inc=1, device_id=device, device_id_type=MESH)

    loads = [
        pltpu.make_async_copy(source, own.at[side], load_sem.at[side])
        for side, source in enumerate((lstate, rstate))
    ]
    for load in loads:
        load.start()
    pl.semaphore_wait(barrier, len(greeted))

    def rows(step):
        return pl.ds(pl.multiple_of(step * STEP_ROWS, STEP_ROWS), STEP_ROWS)

    def x_copy(side, step):
        return pltpu.make_async_remote_copy(
            (lenv, renv)[side].at[:, rows(step), :],
            env.at[side, 0, :, rows(step), :],
            x_send.at[side, step], x_recv.at[side, step],
            device_id=(ahead, behind)[side], device_id_type=MESH,
        )

    def y_copy(side, step):
        return pltpu.make_async_remote_copy(
            env.at[side, 0, :, rows(step), :],
            env.at[side, 2, :, rows(step), :],
            y_send.at[side, step], y_recv.at[side, step],
            device_id=(at(0, 2), at(0, -2))[side], device_id_type=MESH,
        )

    def d_copy(side, step):
        held = (2 * core, 2 * (1 - core))[side]
        return pltpu.make_async_remote_copy(
            env.at[side, held, :, rows(step), :],
            env.at[side, 1, :, rows(step), :],
            d_send.at[side, step], d_recv.at[side, step],
            device_id=partner, device_id_type=MESH,
        )

    def s_copy(n):
        side, first, count, device = (
            (0, 0, 4, ahead), (1, 0, 1, behind), (1, 1, 2, at(-1, -1)), (1, 3, 1, at(-1, -2)),
        )[n]
        return pltpu.make_async_remote_copy(
            own.at[side, pl.ds(first, count)],
            site.at[side, pl.ds(first, count)],
            s_send.at[n], s_recv.at[n],
            device_id=device, device_id_type=MESH,
        )

    for side in range(2):
        x_copy(side, 0).start()

    for load in loads:
        load.wait()
    row_ids = lax.broadcasted_iota(jnp.int32, (slot, slot), 0)
    col_ids = lax.broadcasted_iota(jnp.int32, (slot, slot), 1)
    for s in range(4):
        source = k - OFFSETS[s]
        live = jnp.where(source >= 0, sizes[jnp.maximum(source, 0)], 0)
        live = jnp.where(couple[s] > 0, live, 0)
        keep = (row_ids < live) & (col_ids < sizes[k])
        own[0, s] = jnp.where(keep, own[0, s].astype(F32), 0.0).astype(BF)
        own[1, s] = jnp.where(keep, own[1, s].astype(F32), 0.0).T.astype(BF)
    for n in range(4):
        s_copy(n).start()
    for side in range(2):
        x_copy(side, 1).start()

    def picker(count, first):
        shape = (count * TILE, mixers.shape[2])
        r = lax.broadcasted_iota(jnp.int32, shape, 0)
        c = lax.broadcasted_iota(jnp.int32, shape, 1)
        return jnp.where(r // TILE + first == c, 1.0, 0.0).astype(BF)

    def spread(side, count, first):
        pick = picker(count, first)
        part = jnp.dot(pick, mixers[side], preferred_element_type=F32).astype(BF)
        full = transposed_dot(part, pick)
        r = lax.broadcasted_iota(jnp.int32, full.shape, 0)
        c = lax.broadcasted_iota(jnp.int32, full.shape, 1)
        return jnp.where(lax.rem(r, TILE) == lax.rem(c, TILE), full, 0.0).astype(BF)

    for side in range(2):
        mix0[side] = spread(side, width, 0)
        mix3[side] = spread(side, width, 3 * width)
        mix12[side] = spread(side, 2 * width, width)

    def clear(v, carry):
        for side in range(2):
            total[side, v] = jnp.zeros((slot, slot), F32)
        return carry

    lax.fori_loop(0, width, clear, 0)

    def turn():
        for n in range(4):
            s_copy(n).wait_recv()
        for side in range(2):
            for q in range(quarters):
                part = site[side, :, q * UNIT_ROWS : (q + 1) * UNIT_ROWS, :]
                turned[side, q] = part.reshape(4 * UNIT_ROWS, slot).astype(F32).T.astype(BF)

    def unit(side, q):
        span = pl.ds(pl.multiple_of(q * UNIT_ROWS, UNIT_ROWS), UNIT_ROWS)

        def first(s, carry):
            held = env[side, (s + 1) // 2, :, span, :].reshape(width * UNIT_ROWS, slot)
            product = jnp.dot(held, site[side, s], preferred_element_type=F32)
            inner[s] = product.astype(BF).reshape(width, UNIT_ROWS, slot)
            return carry

        lax.fori_loop(0, 4, first, 0)

        def mix(a, carry):
            part = pl.ds(pl.multiple_of(a * TILE, TILE), TILE)
            for s, weights in ((0, mix0), (3, mix3)):
                held = inner[s, :, part, :].reshape(width * TILE, slot)
                product = jnp.dot(weights[side], held, preferred_element_type=F32)
                mixed[:, s, part, :] = product.astype(BF).reshape(width, TILE, slot)
            held = inner[1:3, :, part, :].reshape(2 * width * TILE, slot)
            product = jnp.dot(mix12[side], held, preferred_element_type=F32)
            product = product.astype(BF).reshape(2, width, TILE, slot)
            mixed[:, 1, part, :] = product[0]
            mixed[:, 2, part, :] = product[1]
            return carry

        lax.fori_loop(0, UNIT_ROWS // TILE, mix, 0)

        def last(v, carry):
            held = mixed[v].reshape(4 * UNIT_ROWS, slot)
            value = total[side, v] + jnp.dot(turned[side, q], held, preferred_element_type=F32)
            total[side, v] = value
            result[side, v] = value.astype(BF)
            return carry

        lax.fori_loop(0, width, last, 0)

    per_unit = UNIT_ROWS // STEP_ROWS

    def step(c, carry):
        @pl.when(c < steps)
        def _():
            for side in range(2):
                x_copy(side, c).wait_recv()
                y_copy(side, c).start()
                x_copy(side, c).wait_send()

        @pl.when(c + 2 < steps)
        def _():
            for side in range(2):
                x_copy(side, c + 2).start()

        @pl.when((c >= 1) & (c <= steps))
        def _():
            for side in range(2):
                y_copy(side, c - 1).wait_recv()
                d_copy(side, c - 1).start()

        @pl.when(c == per_unit)
        def _():
            turn()

        @pl.when(c >= per_unit + 1)
        def _():
            u = c - per_unit - 1
            side, q = lax.rem(u, 2), u // 2
            for part in range(per_unit):
                @pl.when(side == 0)
                def _():
                    d_copy(0, q * per_unit + part).wait_recv()

                @pl.when(side == 1)
                def _():
                    d_copy(1, q * per_unit + part).wait_recv()
            unit(side, q)

        return carry

    lax.fori_loop(0, 2 * quarters + per_unit + 1, step, 0)

    for side, (edge, source, target) in enumerate(((0, lenv, lout), (chains - 1, renv, rout))):
        @pl.when(i == edge)
        def _():
            pltpu.make_async_copy(source, target, out_sem.at[side]).start()

        @pl.when(i != edge)
        def _():
            pltpu.make_async_copy(result.at[side], target, out_sem.at[side]).start()

    for n in range(4):
        s_copy(n).wait_send()

    def settle(c, carry):
        for side in range(2):
            y_copy(side, c).wait_send()
            d_copy(side, c).wait_send()
        return carry

    lax.fori_loop(0, steps, settle, 0)
    for side, target in enumerate((lout, rout)):
        pltpu.make_async_copy(result.at[side], target, out_sem.at[side]).wait()


def body(chains, sectors, left_env, right_env, left_state, right_state, mpo, couple, sizes):
    width, slot = left_env.shape[2], left_env.shape[3]
    steps, quarters = slot // STEP_ROWS, slot // UNIT_ROWS
    mixers = jnp.stack(
        [
            jnp.transpose(mpo, (1, 3, 2, 0)).reshape(4 * width, 4 * width),
            jnp.transpose(mpo, (1, 0, 2, 3)).reshape(4 * width, 4 * width),
        ]
    )
    anywhere = pl.BlockSpec(memory_space=pl.ANY)
    scalars = pl.BlockSpec(memory_space=pltpu.SMEM)
    dma = pltpu.SemaphoreType.DMA

    def run(*refs):
        kernel(chains, sectors, *refs)

    flops = 2 * 2 * width * slot * slot * (8 * slot + 6 * width)
    left_out, right_out = pl.pallas_call(
        run,
        out_shape=[jax.ShapeDtypeStruct((width, slot, slot), BF)] * 2,
        in_specs=[anywhere] * 4 + [pl.BlockSpec(memory_space=pltpu.VMEM), scalars, scalars],
        out_specs=[anywhere] * 2,
        scratch_shapes=[
            pltpu.VMEM((2, 3, width, slot, slot), BF),
            pltpu.VMEM((2, 4, slot, slot), BF),
            pltpu.VMEM((2, 4, slot, slot), BF),
            pltpu.VMEM((2, quarters, slot, 4 * UNIT_ROWS), BF),
            pltpu.VMEM((2, width * TILE, width * TILE), BF),
            pltpu.VMEM((2, width * TILE, width * TILE), BF),
            pltpu.VMEM((2, 2 * width * TILE, 2 * width * TILE), BF),
            pltpu.VMEM((4, width, UNIT_ROWS, slot), BF),
            pltpu.VMEM((width, 4, UNIT_ROWS, slot), BF),
            pltpu.VMEM((2, width, slot, slot), F32),
            pltpu.VMEM((2, width, slot, slot), BF),
            dma((2,)),
            dma((2, steps)), dma((2, steps)),
            dma((2, steps)), dma((2, steps)),
            dma((2, steps)), dma((2, steps)),
            dma((4,)), dma((4,)),
            dma((2,)),
        ],
        compiler_params=pltpu.CompilerParams(
            collective_id=0, has_side_effects=True, vmem_limit_bytes=60 << 20
        ),
        cost_estimate=pl.CostEstimate(flops=flops, bytes_accessed=10 << 20, transcendentals=0),
    )(
        left_env[0, 0], right_env[0, 0], left_state[0, 0], right_state[0, 0],
        mixers, couple[0, :, 0], sizes,
    )
    return left_out[None, None], right_out[None, None]


def solution(mesh):
    blocks = P("chain", "sector", None, None, None)
    chains, sectors = mesh.shape["chain"], mesh.shape["sector"]

    def run(*args):
        return body(chains, sectors, *args)

    return jax.shard_map(
        run,
        mesh=mesh,
        in_specs=(blocks, blocks, blocks, blocks, P(), P("chain", None, "sector"), P()),
        out_specs=(blocks, blocks),
        check_vma=False,
    )
```

```python
import jax
import jax.numpy as jnp
from jax import lax
from jax.experimental import pallas as pl
from jax.experimental.pallas import tpu as pltpu
from jax.sharding import PartitionSpec as P

MESH = pl.DeviceIdType.MESH
BF = jnp.bfloat16
F32 = jnp.float32
OFFSETS = (0, 1, 1, 2)
STEP_ROWS = 32
UNIT_ROWS = 32
DEPTH = 2
TILE = 16


def transposed_dot(a, b):
    return lax.dot_general(a, b, (((1,), (1,)), ((), ())), preferred_element_type=F32)


def kernel(
    chains, sectors,
    lenv, renv, lstate, rstate, mpo, couple, sizes,
    lout, rout,
    env, own, site, turned, mix0, mix3, mix12, inner, mixed, total, result, kept,
    load_sem, x_send, x_recv, y_send, y_recv, d_send, d_recv, s_send, s_recv, kept_sem, out_sem,
):
    width, slot = lenv.shape[0], lenv.shape[1]
    steps, quarters = slot // STEP_ROWS, slot // UNIT_ROWS
    i = lax.axis_index("chain")
    k = lax.axis_index("sector")
    core = lax.rem(k, 2)

    def at(chain_step, sector_step):
        return (
            lax.rem(i + chain_step + chains, chains),
            lax.rem(k + sector_step + sectors, sectors),
        )

    partner = (i, k + 1 - 2 * core)
    ahead, behind = at(1, 0), at(-1, 0)
    barrier = pltpu.get_barrier_semaphore()
    greeted = (
        ahead, behind, at(0, 2), at(0, -2), partner,
        at(-1, -1), at(-1, -2), at(1, 1), at(1, 2),
    )
    for device in greeted:
        pl.semaphore_signal(barrier, inc=1, device_id=device, device_id_type=MESH)

    loads = [
        pltpu.make_async_copy(source, own.at[side], load_sem.at[side])
        for side, source in enumerate((lstate, rstate))
    ]
    for load in loads:
        load.start()
    pl.semaphore_wait(barrier, len(greeted))

    def rows(step):
        return pl.ds(pl.multiple_of(step * STEP_ROWS, STEP_ROWS), STEP_ROWS)

    def x_copy(side, step):
        return pltpu.make_async_remote_copy(
            (lenv, renv)[side].at[:, rows(step), :],
            env.at[side, 0, :, rows(step), :],
            x_send.at[side, step], x_recv.at[side, step],
            device_id=(ahead, behind)[side], device_id_type=MESH,
        )

    def y_copy(side, step):
        return pltpu.make_async_remote_copy(
            env.at[side, 0, :, rows(step), :],
            env.at[side, 2, :, rows(step), :],
            y_send.at[side, step], y_recv.at[side, step],
            device_id=(at(0, 2), at(0, -2))[side], device_id_type=MESH,
        )

    def d_copy(side, step):
        held = (2 * core, 2 * (1 - core))[side]
        return pltpu.make_async_remote_copy(
            env.at[side, held, :, rows(step), :],
            env.at[side, 1, :, rows(step), :],
            d_send.at[side, step], d_recv.at[side, step],
            device_id=partner, device_id_type=MESH,
        )

    def d_wait(side, step):
        pltpu.make_async_remote_copy(
            env.at[side, 0, :, rows(step), :],
            env.at[side, 1, :, rows(step), :],
            d_send.at[side, step], d_recv.at[side, step],
            device_id=partner, device_id_type=MESH,
        ).wait_recv()

    def s_copy(n):
        side, first, count, device = (
            (0, 0, 4, ahead), (1, 0, 1, behind), (1, 1, 2, at(-1, -1)), (1, 3, 1, at(-1, -2)),
        )[n]
        return pltpu.make_async_remote_copy(
            own.at[side, pl.ds(first, count)],
            site.at[side, pl.ds(first, count)],
            s_send.at[n], s_recv.at[n],
            device_id=device, device_id_type=MESH,
        )

    for side in range(2):
        x_copy(side, 0).start()

    edges = ((0, lenv, lout), (chains - 1, renv, rout))

    def keep_copy(side):
        return pltpu.make_async_copy(edges[side][1], kept.at[side], kept_sem.at[side])

    for side in range(2):
        @pl.when(i == edges[side][0])
        def _():
            keep_copy(side).start()

    for load in loads:
        load.wait()
    row_ids = lax.broadcasted_iota(jnp.int32, (slot, slot), 0)
    col_ids = lax.broadcasted_iota(jnp.int32, (slot, slot), 1)
    for s in range(4):
        source = k - OFFSETS[s]
        live = jnp.where(source >= 0, sizes[jnp.maximum(source, 0)], 0)
        live = jnp.where(couple[s] > 0, live, 0)
        keep = (row_ids < live) & (col_ids < sizes[k])
        own[0, s] = jnp.where(keep, own[0, s].astype(F32), 0.0).astype(BF)
        own[1, s] = jnp.where(keep, own[1, s].astype(F32), 0.0).T.astype(BF)
    for n in range(4):
        s_copy(n).start()
    for n in range(1, DEPTH):
        for side in range(2):
            x_copy(side, n).start()

    def picker(count, member):
        shape = (count * width * TILE, width)
        r = lax.broadcasted_iota(jnp.int32, shape, 0)
        c = lax.broadcasted_iota(jnp.int32, shape, 1)
        return jnp.where(r // TILE == c + member * width, 1.0, 0.0).astype(BF)

    def entries(s, t):
        r = lax.broadcasted_iota(jnp.int32, (width, width), 0)
        found = jnp.zeros((width, width), F32)
        for w in range(width):
            line = mpo[w, s].astype(F32)[t : t + 1, :]
            found = jnp.where(r == w, jnp.broadcast_to(line, (width, width)), found)
        return found.astype(BF)

    def spread(side, members):
        count = len(members)
        picks = [picker(count, n) for n in range(count)]
        full = jnp.zeros((count * width * TILE, count * width * TILE), F32)
        for n in range(count):
            part = jnp.zeros((count * width * TILE, width), F32)
            for m in range(count):
                pair = (members[n], members[m]) if side == 0 else (members[m], members[n])
                part += jnp.dot(picks[m], entries(*pair), preferred_element_type=F32)
            part = part.astype(BF)
            full += transposed_dot(picks[n], part) if side == 0 else transposed_dot(part, picks[n])
        r = lax.broadcasted_iota(jnp.int32, full.shape, 0)
        c = lax.broadcasted_iota(jnp.int32, full.shape, 1)
        return jnp.where(lax.rem(r, TILE) == lax.rem(c, TILE), full, 0.0).astype(BF)

    for side in range(2):
        mix0[side] = spread(side, (0,))
        mix3[side] = spread(side, (3,))
        mix12[side] = spread(side, (1, 2))

    def clear(v, carry):
        for side in range(2):
            total[side, v] = jnp.zeros((slot, slot), F32)
        return carry

    lax.fori_loop(0, width, clear, 0)

    def turn():
        for n in range(4):
            s_copy(n).wait_recv()
        for side in range(2):
            for q in range(quarters):
                part = site[side, :, q * UNIT_ROWS : (q + 1) * UNIT_ROWS, :]
                turned[side, q] = part.reshape(4 * UNIT_ROWS, slot).astype(F32).T.astype(BF)

    def unit(side, q):
        span = pl.ds(pl.multiple_of(q * UNIT_ROWS, UNIT_ROWS), UNIT_ROWS)

        def first(s, carry):
            held = env[side, (s + 1) // 2, :, span, :].reshape(width * UNIT_ROWS, slot)
            product = jnp.dot(held, site[side, s], preferred_element_type=F32)
            inner[s] = product.astype(BF).reshape(width, UNIT_ROWS, slot)
            return carry

        lax.fori_loop(0, 4, first, 0, unroll=True)

        def mix(a, carry):
            part = pl.ds(pl.multiple_of(a * TILE, TILE), TILE)
            for s, weights in ((0, mix0), (3, mix3)):
                held = inner[s, :, part, :].reshape(width * TILE, slot)
                product = jnp.dot(weights[side], held, preferred_element_type=F32)
                mixed[:, s, part, :] = product.astype(BF).reshape(width, TILE, slot)
            held = inner[1:3, :, part, :].reshape(2 * width * TILE, slot)
            product = jnp.dot(mix12[side], held, preferred_element_type=F32)
            product = product.astype(BF).reshape(2, width, TILE, slot)
            mixed[:, 1, part, :] = product[0]
            mixed[:, 2, part, :] = product[1]
            return carry

        lax.fori_loop(0, UNIT_ROWS // TILE, mix, 0, unroll=True)

        def last(v, carry):
            held = mixed[v].reshape(4 * UNIT_ROWS, slot)
            value = total[side, v] + jnp.dot(turned[side, q], held, preferred_element_type=F32)
            total[side, v] = value
            result[side, v] = value.astype(BF)
            return carry

        lax.fori_loop(0, width, last, 0, unroll=True)

    per_unit = UNIT_ROWS // STEP_ROWS

    def step(c, carry):
        @pl.when(c < steps)
        def _():
            for side in range(2):
                x_copy(side, c).wait_recv()
                y_copy(side, c).start()
                x_copy(side, c).wait_send()

        @pl.when(c + DEPTH < steps)
        def _():
            for side in range(2):
                x_copy(side, c + DEPTH).start()

        @pl.when((c >= 1) & (c <= steps))
        def _():
            for side in range(2):
                y_copy(side, c - 1).wait_recv()
                d_copy(side, c - 1).start()

        @pl.when(c == per_unit)
        def _():
            turn()

        @pl.when((c > per_unit) & (lax.rem(c, per_unit) == 1 % per_unit))
        def _():
            q = (c - 2) // per_unit

            def one(side, carry):
                for part in range(per_unit):
                    d_wait(side, q * per_unit + part)
                unit(side, q)
                return carry

            lax.fori_loop(0, 2, one, 0)

        return carry

    lax.fori_loop(0, steps + 2, step, 0)

    for side, (edge, source, target) in enumerate(edges):
        @pl.when(i == edge)
        def _():
            keep_copy(side).wait()
            pltpu.make_async_copy(kept.at[side], target, out_sem.at[side]).start()

        @pl.when(i != edge)
        def _():
            pltpu.make_async_copy(result.at[side], target, out_sem.at[side]).start()

    for n in range(4):
        s_copy(n).wait_send()

    def settle(c, carry):
        for side in range(2):
            y_copy(side, c).wait_send()
            d_copy(side, c).wait_send()
        return carry

    lax.fori_loop(0, steps, settle, 0)
    for side, target in enumerate((lout, rout)):
        pltpu.make_async_copy(result.at[side], target, out_sem.at[side]).wait()


def body(chains, sectors, left_env, right_env, left_state, right_state, mpo, couple, sizes):
    width, slot = left_env.shape[2], left_env.shape[3]
    steps, quarters = slot // STEP_ROWS, slot // UNIT_ROWS
    anywhere = pl.BlockSpec(memory_space=pl.ANY)
    scalars = pl.BlockSpec(memory_space=pltpu.SMEM)
    dma = pltpu.SemaphoreType.DMA

    def run(*refs):
        kernel(chains, sectors, *refs)

    flops = 2 * 2 * width * slot * slot * (8 * slot + 6 * width)
    left_out, right_out = pl.pallas_call(
        run,
        out_shape=[jax.ShapeDtypeStruct((width, slot, slot), BF)] * 2,
        in_specs=[anywhere] * 4 + [pl.BlockSpec(memory_space=pltpu.VMEM), scalars, scalars],
        out_specs=[anywhere] * 2,
        scratch_shapes=[
            pltpu.VMEM((2, 3, width, slot, slot), BF),
            pltpu.VMEM((2, 4, slot, slot), BF),
            pltpu.VMEM((2, 4, slot, slot), BF),
            pltpu.VMEM((2, quarters, slot, 4 * UNIT_ROWS), BF),
            pltpu.VMEM((2, width * TILE, width * TILE), BF),
            pltpu.VMEM((2, width * TILE, width * TILE), BF),
            pltpu.VMEM((2, 2 * width * TILE, 2 * width * TILE), BF),
            pltpu.VMEM((4, width, UNIT_ROWS, slot), BF),
            pltpu.VMEM((width, 4, UNIT_ROWS, slot), BF),
            pltpu.VMEM((2, width, slot, slot), F32),
            pltpu.VMEM((2, width, slot, slot), BF),
            pltpu.VMEM((2, width, slot, slot), BF),
            dma((2,)),
            dma((2, steps)), dma((2, steps)),
            dma((2, steps)), dma((2, steps)),
            dma((2, steps)), dma((2, steps)),
            dma((4,)), dma((4,)),
            dma((2,)), dma((2,)),
        ],
        compiler_params=pltpu.CompilerParams(
            collective_id=0, has_side_effects=True, vmem_limit_bytes=60 << 20
        ),
        cost_estimate=pl.CostEstimate(flops=flops, bytes_accessed=10 << 20, transcendentals=0),
    )(
        left_env[0, 0], right_env[0, 0], left_state[0, 0], right_state[0, 0],
        mpo, couple[0, :, 0], sizes,
    )
    return left_out[None, None], right_out[None, None]


def solution(mesh):
    blocks = P("chain", "sector", None, None, None)
    chains, sectors = mesh.shape["chain"], mesh.shape["sector"]

    def run(*args):
        return body(chains, sectors, *args)

    return jax.shard_map(
        run,
        mesh=mesh,
        in_specs=(blocks, blocks, blocks, blocks, P(), P("chain", None, "sector"), P()),
        out_specs=(blocks, blocks),
        check_vma=False,
    )
```

```python
import jax
import jax.numpy as jnp
from jax import lax
from jax.experimental import pallas as pl
from jax.experimental.pallas import tpu as pltpu
from jax.sharding import PartitionSpec as P

MESH = pl.DeviceIdType.MESH
BF = jnp.bfloat16
F32 = jnp.float32
OFFSETS = (0, 1, 1, 2)
STEP_ROWS = 32
UNIT_ROWS = STEP_ROWS
STATES = ((0,), (1, 2, 3))
TILE = 16


def transposed_dot(a, b):
    return lax.dot_general(a, b, (((1,), (1,)), ((), ())), preferred_element_type=F32)


def kernel(
    chains, sectors,
    lenv, renv, lstate, rstate, mpo, couple, sizes,
    result,
    env, own, site, turned, mix0, mix3, mix12, inner, mixed, total,
    load_sem, x_send, x_recv, y_send, y_recv, d_send, d_recv, s_send, s_recv, edge_sem,
):
    width, slot = lenv.shape[0], lenv.shape[1]
    steps, units = slot // STEP_ROWS, slot // UNIT_ROWS
    i = lax.axis_index("chain")
    k = lax.axis_index("sector")
    core = lax.rem(k, 2)

    def at(chain_step, sector_step):
        return (
            lax.rem(i + chain_step + chains, chains),
            lax.rem(k + sector_step + sectors, sectors),
        )

    partner = (i, k + 1 - 2 * core)
    ahead, behind = at(1, 0), at(-1, 0)
    barrier = pltpu.get_barrier_semaphore()
    gets = (i > 0, i < chains - 1)
    gives = (gets[1], gets[0])

    def greet(*devices):
        for device in devices:
            pl.semaphore_signal(barrier, inc=1, device_id=device, device_id_type=MESH)

    greet(at(0, 2), at(0, -2), partner)

    @pl.when(gives[0])
    def _():
        greet(ahead, at(1, 1), at(1, 2))

    @pl.when(gives[1])
    def _():
        greet(behind, at(-1, -1), at(-1, -2))


    loads = [
        pltpu.make_async_copy(source, own.at[side], load_sem.at[side])
        for side, source in enumerate((lstate, rstate))
    ]
    for load in loads:
        load.start()
    ends = jnp.where(i == 0, 1, 0) + jnp.where(i == chains - 1, 1, 0)
    pl.semaphore_wait(barrier, 9 - 3 * ends)

    def rows(step):
        return pl.ds(pl.multiple_of(step * STEP_ROWS, STEP_ROWS), STEP_ROWS)

    def x_copy(side, step):
        return pltpu.make_async_remote_copy(
            (lenv, renv)[side].at[:, rows(step), :],
            env.at[side, 0, :, rows(step), :],
            x_send.at[side, step], x_recv.at[side, step],
            device_id=(ahead, behind)[side], device_id_type=MESH,
        )

    def y_copy(side, step):
        return pltpu.make_async_remote_copy(
            env.at[side, 0, :, rows(step), :],
            env.at[side, 2, :, rows(step), :],
            y_send.at[side, step], y_recv.at[side, step],
            device_id=(at(0, 2), at(0, -2))[side], device_id_type=MESH,
        )

    def d_copy(side, step):
        held = (2 * core, 2 * (1 - core))[side]
        return pltpu.make_async_remote_copy(
            env.at[side, held, :, rows(step), :],
            env.at[side, 1, :, rows(step), :],
            d_send.at[side, step], d_recv.at[side, step],
            device_id=partner, device_id_type=MESH,
        )

    def d_wait(side, step):
        pltpu.make_async_remote_copy(
            env.at[side, 0, :, rows(step), :],
            env.at[side, 1, :, rows(step), :],
            d_send.at[side, step], d_recv.at[side, step],
            device_id=partner, device_id_type=MESH,
        ).wait_recv()

    def s_copy(n):
        side, first, count, device = (
            (0, 0, 4, ahead), (1, 0, 1, behind), (1, 1, 2, at(-1, -1)), (1, 3, 1, at(-1, -2)),
        )[n]
        return pltpu.make_async_remote_copy(
            own.at[side, pl.ds(first, count)],
            site.at[side, pl.ds(first, count)],
            s_send.at[n], s_recv.at[n],
            device_id=device, device_id_type=MESH,
        )

    edges = ((0, lenv), (chains - 1, renv))

    def edge_copy(side):
        return pltpu.make_async_copy(edges[side][1], result.at[side], edge_sem.at[side])

    for side in range(2):
        @pl.when(gives[side])
        def _():
            x_copy(side, 0).start()

        @pl.when(i == edges[side][0])
        def _():
            edge_copy(side).start()

    for load in loads:
        load.wait()
    row_ids = lax.broadcasted_iota(jnp.int32, (slot, slot), 0)
    col_ids = lax.broadcasted_iota(jnp.int32, (slot, slot), 1)
    for s in range(4):
        source = k - OFFSETS[s]
        live = jnp.where(source >= 0, sizes[jnp.maximum(source, 0)], 0)
        live = jnp.where(couple[s] > 0, live, 0)
        keep = (row_ids < live) & (col_ids < sizes[k])
        own[0, s] = jnp.where(keep, own[0, s].astype(F32), 0.0).astype(BF)
        own[1, s] = jnp.where(keep, own[1, s].astype(F32), 0.0).T.astype(BF)
    for side in range(2):
        @pl.when(gives[side])
        def _():
            for n in STATES[side]:
                s_copy(n).start()

    def send(n, carry):
        for side in range(2):
            @pl.when(gives[side])
            def _():
                x_copy(side, n).start()
        return carry

    lax.fori_loop(1, steps, send, 0)

    def picker(count, member):
        shape = (count * width * TILE, width)
        r = lax.broadcasted_iota(jnp.int32, shape, 0)
        c = lax.broadcasted_iota(jnp.int32, shape, 1)
        return jnp.where(r // TILE == c + member * width, 1.0, 0.0).astype(BF)

    def entries(s, t):
        r = lax.broadcasted_iota(jnp.int32, (width, width), 0)
        found = jnp.zeros((width, width), F32)
        for w in range(width):
            line = mpo[w, s].astype(F32)[t : t + 1, :]
            found = jnp.where(r == w, jnp.broadcast_to(line, (width, width)), found)
        return found.astype(BF)

    def spread(side, members):
        count = len(members)
        picks = [picker(count, n) for n in range(count)]
        full = jnp.zeros((count * width * TILE, count * width * TILE), F32)
        for n in range(count):
            part = jnp.zeros((count * width * TILE, width), F32)
            for m in range(count):
                pair = (members[n], members[m]) if side == 0 else (members[m], members[n])
                part += jnp.dot(picks[m], entries(*pair), preferred_element_type=F32)
            part = part.astype(BF)
            full += transposed_dot(picks[n], part) if side == 0 else transposed_dot(part, picks[n])
        r = lax.broadcasted_iota(jnp.int32, full.shape, 0)
        c = lax.broadcasted_iota(jnp.int32, full.shape, 1)
        return jnp.where(lax.rem(r, TILE) == lax.rem(c, TILE), full, 0.0).astype(BF)

    for side in range(2):
        mix0[side] = spread(side, (0,))
        mix3[side] = spread(side, (3,))
        mix12[side] = spread(side, (1, 2))

    def clear(v, carry):
        for side in range(2):
            total[side, v] = jnp.zeros((slot, slot), F32)
        return carry

    lax.fori_loop(0, width, clear, 0)

    def turn():
        for side in range(2):
            @pl.when(gets[side])
            def _():
                for n in STATES[side]:
                    s_copy(n).wait_recv()
                for q in range(units):
                    part = site[side, :, q * UNIT_ROWS : (q + 1) * UNIT_ROWS, :]
                    turned[side, q] = part.reshape(4 * UNIT_ROWS, slot).astype(F32).T.astype(BF)

    def unit(side, q):
        span = pl.ds(pl.multiple_of(q * UNIT_ROWS, UNIT_ROWS), UNIT_ROWS)
        for s in range(4):
            held = env[side, (s + 1) // 2, :, span, :].reshape(width * UNIT_ROWS, slot)
            product = jnp.dot(held, site[side, s], preferred_element_type=F32)
            inner[s] = product.astype(BF).reshape(width, UNIT_ROWS, slot)
        for a in range(UNIT_ROWS // TILE):
            part = pl.ds(a * TILE, TILE)
            for s, weights in ((0, mix0), (3, mix3)):
                held = inner[s, :, part, :].reshape(width * TILE, slot)
                product = jnp.dot(weights[side], held, preferred_element_type=F32)
                mixed[:, s, part, :] = product.astype(BF).reshape(width, TILE, slot)
            held = inner[1:3, :, part, :].reshape(2 * width * TILE, slot)
            product = jnp.dot(mix12[side], held, preferred_element_type=F32)
            product = product.astype(BF).reshape(2, width, TILE, slot)
            mixed[:, 1, part, :] = product[0]
            mixed[:, 2, part, :] = product[1]
        for v in range(width):
            held = mixed[v].reshape(4 * UNIT_ROWS, slot)
            value = total[side, v] + jnp.dot(turned[side, q], held, preferred_element_type=F32)
            total[side, v] = value
            result[side, v] = value.astype(BF)

    def got(side):
        return jnp.where(side == 0, i, chains - 1 - i) > 0

    def step(c, carry):
        for side in range(2):
            @pl.when((c < steps) & gets[side])
            def _():
                x_copy(side, c).wait_recv()
                y_copy(side, c).start()

        for side in range(2):
            @pl.when((c >= 1) & (c <= steps) & gets[side])
            def _():
                y_copy(side, c - 1).wait_recv()
                d_copy(side, c - 1).start()

        @pl.when(c == 1)
        def _():
            turn()

        @pl.when(c >= 2)
        def _():
            def one(side, carry):
                @pl.when(got(side))
                def _():
                    d_wait(side, c - 2)
                    unit(side, c - 2)

                return carry

            lax.fori_loop(0, 2, one, 0)

        return carry

    lax.fori_loop(0, steps + 2, step, 0)

    def settle(c, carry):
        for side in range(2):
            @pl.when(gives[side])
            def _():
                x_copy(side, c).wait_send()

            @pl.when(gets[side])
            def _():
                y_copy(side, c).wait_send()
                d_copy(side, c).wait_send()
        return carry

    lax.fori_loop(0, steps, settle, 0)
    for side in range(2):
        @pl.when(gives[side])
        def _():
            for n in STATES[side]:
                s_copy(n).wait_send()

        @pl.when(i == edges[side][0])
        def _():
            edge_copy(side).wait()


def body(chains, sectors, left_env, right_env, left_state, right_state, mpo, couple, sizes):
    width, slot = left_env.shape[2], left_env.shape[3]
    steps, units = slot // STEP_ROWS, slot // UNIT_ROWS
    anywhere = pl.BlockSpec(memory_space=pl.ANY)
    scalars = pl.BlockSpec(memory_space=pltpu.SMEM)
    dma = pltpu.SemaphoreType.DMA

    def run(*refs):
        kernel(chains, sectors, *refs)

    flops = 2 * 2 * width * slot * slot * (8 * slot + 6 * width)
    out = pl.pallas_call(
        run,
        out_shape=pltpu.VMEM((2, width, slot, slot), BF),
        in_specs=[anywhere] * 4 + [pl.BlockSpec(memory_space=pltpu.VMEM), scalars, scalars],
        out_specs=pl.BlockSpec(memory_space=pltpu.VMEM),
        scratch_shapes=[
            pltpu.VMEM((2, 3, width, slot, slot), BF),
            pltpu.VMEM((2, 4, slot, slot), BF),
            pltpu.VMEM((2, 4, slot, slot), BF),
            pltpu.VMEM((2, units, slot, 4 * UNIT_ROWS), BF),
            pltpu.VMEM((2, width * TILE, width * TILE), BF),
            pltpu.VMEM((2, width * TILE, width * TILE), BF),
            pltpu.VMEM((2, 2 * width * TILE, 2 * width * TILE), BF),
            pltpu.VMEM((4, width, UNIT_ROWS, slot), BF),
            pltpu.VMEM((width, 4, UNIT_ROWS, slot), BF),
            pltpu.VMEM((2, width, slot, slot), F32),
            dma((2,)),
            dma((2, steps)), dma((2, steps)),
            dma((2, steps)), dma((2, steps)),
            dma((2, steps)), dma((2, steps)),
            dma((4,)), dma((4,)),
            dma((2,)),
        ],
        compiler_params=pltpu.CompilerParams(
            collective_id=0, has_side_effects=True, vmem_limit_bytes=60 << 20
        ),
        cost_estimate=pl.CostEstimate(flops=flops, bytes_accessed=10 << 20, transcendentals=0),
    )(
        left_env[0, 0], right_env[0, 0], left_state[0, 0], right_state[0, 0],
        mpo, couple[0, :, 0], sizes,
    )
    return out[0][None, None], out[1][None, None]


def solution(mesh):
    blocks = P("chain", "sector", None, None, None)
    chains, sectors = mesh.shape["chain"], mesh.shape["sector"]

    def run(*args):
        return body(chains, sectors, *args)

    return jax.shard_map(
        run,
        mesh=mesh,
        in_specs=(blocks, blocks, blocks, blocks, P(), P("chain", None, "sector"), P()),
        out_specs=(blocks, blocks),
        check_vma=False,
    )
```

```python
import jax
import jax.numpy as jnp
from jax import lax
from jax.experimental import pallas as pl
from jax.experimental.pallas import tpu as pltpu
from jax.sharding import PartitionSpec as P

MESH = pl.DeviceIdType.MESH
BF = jnp.bfloat16
F32 = jnp.float32
OFFSETS = (0, 1, 1, 2)
STEP_ROWS = 32
UNIT_ROWS = 32
LAG = 1
STATES = ((0,), (1, 2, 3))
TILE = 16
PARTS = 2
HALF = 8


def transposed_dot(a, b):
    return lax.dot_general(a, b, (((1,), (1,)), ((), ())), preferred_element_type=F32)


def kernel(
    chains, sectors,
    lenv, renv, lstate, rstate, mpo, couple, sizes,
    result,
    env, own, site, turned, mix0, mix3, mix12, inner, mixed, total,
    load_sem, x_send, x_recv, y_send, y_recv, d_send, d_recv, s_send, s_recv, edge_sem,
):
    width, slot = lenv.shape[0], lenv.shape[1]
    steps, units = slot // STEP_ROWS, slot // UNIT_ROWS
    i = lax.axis_index("chain")
    k = lax.axis_index("sector")
    core = lax.rem(k, 2)

    def at(chain_step, sector_step):
        return (
            lax.rem(i + chain_step + chains, chains),
            lax.rem(k + sector_step + sectors, sectors),
        )

    partner = (i, k + 1 - 2 * core)
    ahead, behind = at(1, 0), at(-1, 0)
    barrier = pltpu.get_barrier_semaphore()
    gets = (i > 0, i < chains - 1)
    gives = (gets[1], gets[0])

    def greet(*devices):
        for device in devices:
            pl.semaphore_signal(barrier, inc=1, device_id=device, device_id_type=MESH)

    greet(at(0, 2), at(0, -2), partner)

    @pl.when(gives[0])
    def _():
        greet(ahead, at(1, 1), at(1, 2))

    @pl.when(gives[1])
    def _():
        greet(behind, at(-1, -1), at(-1, -2))


    loads = [
        pltpu.make_async_copy(source, own.at[side], load_sem.at[side])
        for side, source in enumerate((lstate, rstate))
    ]
    for load in loads:
        load.start()
    ends = jnp.where(i == 0, 1, 0) + jnp.where(i == chains - 1, 1, 0)
    pl.semaphore_wait(barrier, 9 - 3 * ends)

    def rows(step):
        return pl.ds(pl.multiple_of(step * STEP_ROWS, STEP_ROWS), STEP_ROWS)

    def x_copy(side, step):
        return pltpu.make_async_remote_copy(
            (lenv, renv)[side].at[:, rows(step), :],
            env.at[side, 0, :, rows(step), :],
            x_send.at[side, step], x_recv.at[side, step],
            device_id=(ahead, behind)[side], device_id_type=MESH,
        )

    def y_copy(side, step):
        return pltpu.make_async_remote_copy(
            env.at[side, 0, :, rows(step), :],
            env.at[side, 2, :, rows(step), :],
            y_send.at[side, step], y_recv.at[side, step],
            device_id=(at(0, 2), at(0, -2))[side], device_id_type=MESH,
        )

    def d_copy(side, step):
        held = (2 * core, 2 * (1 - core))[side]
        return pltpu.make_async_remote_copy(
            env.at[side, held, :, rows(step), :],
            env.at[side, 1, :, rows(step), :],
            d_send.at[side, step], d_recv.at[side, step],
            device_id=partner, device_id_type=MESH,
        )

    def d_wait(side, step):
        pltpu.make_async_remote_copy(
            env.at[side, 0, :, rows(step), :],
            env.at[side, 1, :, rows(step), :],
            d_send.at[side, step], d_recv.at[side, step],
            device_id=partner, device_id_type=MESH,
        ).wait_recv()

    def s_copy(n):
        side, first, count, device = (
            (0, 0, 4, ahead), (1, 0, 1, behind), (1, 1, 2, at(-1, -1)), (1, 3, 1, at(-1, -2)),
        )[n]
        return pltpu.make_async_remote_copy(
            own.at[side, pl.ds(first, count)],
            site.at[side, pl.ds(first, count)],
            s_send.at[n], s_recv.at[n],
            device_id=device, device_id_type=MESH,
        )

    edges = ((0, lenv), (chains - 1, renv))

    def edge_copy(side):
        return pltpu.make_async_copy(edges[side][1], result.at[side], edge_sem.at[side])

    for side in range(2):
        @pl.when(gives[side])
        def _():
            x_copy(side, 0).start()

        @pl.when(i == edges[side][0])
        def _():
            edge_copy(side).start()

    for load in loads:
        load.wait()
    row_ids = lax.broadcasted_iota(jnp.int32, (slot, slot), 0)
    col_ids = lax.broadcasted_iota(jnp.int32, (slot, slot), 1)
    for s in range(4):
        source = k - OFFSETS[s]
        live = jnp.where(source >= 0, sizes[jnp.maximum(source, 0)], 0)
        live = jnp.where(couple[s] > 0, live, 0)
        keep = (row_ids < live) & (col_ids < sizes[k])
        own[0, s] = jnp.where(keep, own[0, s].astype(F32), 0.0).astype(BF)
        own[1, s] = jnp.where(keep, own[1, s].astype(F32), 0.0).T.astype(BF)
    for side in range(2):
        @pl.when(gives[side])
        def _():
            for n in STATES[side]:
                s_copy(n).start()

    def send(n, carry):
        for side in range(2):
            @pl.when(gives[side])
            def _():
                x_copy(side, n).start()
        return carry

    lax.fori_loop(1, steps, send, 0)

    def picker(count, member, tile):
        shape = (count * width * tile, width)
        r = lax.broadcasted_iota(jnp.int32, shape, 0)
        c = lax.broadcasted_iota(jnp.int32, shape, 1)
        return jnp.where(r // tile == c + member * width, 1.0, 0.0).astype(BF)

    def entries(s, t):
        r = lax.broadcasted_iota(jnp.int32, (width, width), 0)
        found = jnp.zeros((width, width), F32)
        for w in range(width):
            line = mpo[w, s].astype(F32)[t : t + 1, :]
            found = jnp.where(r == w, jnp.broadcast_to(line, (width, width)), found)
        return found.astype(BF)

    def spread(side, members, tile):
        count = len(members)
        picks = [picker(count, n, tile) for n in range(count)]
        full = jnp.zeros((count * width * tile, count * width * tile), F32)
        for n in range(count):
            part = jnp.zeros((count * width * tile, width), F32)
            for m in range(count):
                pair = (members[n], members[m]) if side == 0 else (members[m], members[n])
                part += jnp.dot(picks[m], entries(*pair), preferred_element_type=F32)
            part = part.astype(BF)
            full += transposed_dot(picks[n], part) if side == 0 else transposed_dot(part, picks[n])
        r = lax.broadcasted_iota(jnp.int32, full.shape, 0)
        c = lax.broadcasted_iota(jnp.int32, full.shape, 1)
        return jnp.where(lax.rem(r, tile) == lax.rem(c, tile), full, 0.0).astype(BF)

    for side in range(2):
        mix0[side] = spread(side, (0,), TILE)
        mix3[side] = spread(side, (3,), TILE)
        mix12[side] = spread(side, (1, 2), HALF)

    def clear(v, carry):
        for side in range(2):
            total[side, v] = jnp.zeros((slot, slot), F32)
        return carry

    lax.fori_loop(0, width, clear, 0)

    def turn():
        for side in range(2):
            @pl.when(gets[side])
            def _():
                for n in STATES[side]:
                    s_copy(n).wait_recv()
                for q in range(units):
                    part = site[side, :, q * UNIT_ROWS : (q + 1) * UNIT_ROWS, :]
                    turned[side, q] = part.reshape(4 * UNIT_ROWS, slot).astype(F32).T.astype(BF)

    def unit(side, q):
        span = pl.ds(pl.multiple_of(q * UNIT_ROWS, UNIT_ROWS), UNIT_ROWS)
        for s in range(4):
            held = env[side, (s + 1) // 2, :, span, :].reshape(width * UNIT_ROWS, slot)
            product = jnp.dot(held, site[side, s], preferred_element_type=F32)
            inner[s] = product.astype(BF).reshape(width, UNIT_ROWS, slot)
        for a in range(UNIT_ROWS // TILE):
            part = pl.ds(a * TILE, TILE)
            for s, weights in ((0, mix0), (3, mix3)):
                held = inner[s, :, part, :].reshape(width * TILE, slot)
                product = jnp.dot(weights[side], held, preferred_element_type=F32)
                mixed[:, s, part, :] = product.astype(BF).reshape(width, TILE, slot)
            held = inner[1:3, :, part, :].astype(F32)
            halves = []
            for h in range(2):
                some = held[:, :, h * HALF : (h + 1) * HALF, :].reshape(2 * width * HALF, slot)
                product = jnp.dot(mix12[side], some.astype(BF), preferred_element_type=F32)
                halves.append(product.reshape(2, width, HALF, slot))
            product = jnp.concatenate(halves, axis=2).astype(BF)
            mixed[:, 1, part, :] = product[0]
            mixed[:, 2, part, :] = product[1]
        for v in range(width):
            held = mixed[v].reshape(4 * UNIT_ROWS, slot)
            value = total[side, v] + jnp.dot(turned[side, q], held, preferred_element_type=F32)
            total[side, v] = value
            result[side, v] = value.astype(BF)

    def got(side):
        return jnp.where(side == 0, i, chains - 1 - i) > 0

    per_unit = UNIT_ROWS // STEP_ROWS

    def step(c, carry):
        for side in range(2):
            @pl.when((c < steps) & gets[side])
            def _():
                x_copy(side, c).wait_recv()
                y_copy(side, c).start()

        for side in range(2):
            @pl.when((c >= LAG) & (c < steps + LAG) & gets[side])
            def _():
                y_copy(side, c - LAG).wait_recv()
                d_copy(side, c - LAG).start()

        @pl.when(c == 1)
        def _():
            turn()

        @pl.when((c >= per_unit + LAG) & (lax.rem(c - LAG, per_unit) == 0))
        def _():
            q = (c - LAG) // per_unit - 1

            def one(side, carry):
                @pl.when(got(side))
                def _():
                    for part in range(per_unit):
                        d_wait(side, q * per_unit + part)
                    unit(side, q)

                return carry

            lax.fori_loop(0, 2, one, 0)

        return carry

    lax.fori_loop(0, steps + LAG + 1, step, 0)

    def settle(c, carry):
        for side in range(2):
            @pl.when(gives[side])
            def _():
                x_copy(side, c).wait_send()

            @pl.when(gets[side])
            def _():
                y_copy(side, c).wait_send()
                d_copy(side, c).wait_send()
        return carry

    lax.fori_loop(0, steps, settle, 0)
    for side in range(2):
        @pl.when(gives[side])
        def _():
            for n in STATES[side]:
                s_copy(n).wait_send()

        @pl.when(i == edges[side][0])
        def _():
            edge_copy(side).wait()


def write_out(result, lout, rout, sems):
    size = lout.shape[0] // PARTS
    copies = [
        pltpu.make_async_copy(
            result.at[side, pl.ds(part * size, size)], target.at[pl.ds(part * size, size)], sems.at[side, part]
        )
        for part in range(PARTS)
        for side, target in enumerate((lout, rout))
    ]
    for copy in copies:
        copy.start()
    for copy in copies:
        copy.wait()


def body(chains, sectors, left_env, right_env, left_state, right_state, mpo, couple, sizes):
    width, slot = left_env.shape[2], left_env.shape[3]
    steps, units = slot // STEP_ROWS, slot // UNIT_ROWS
    anywhere = pl.BlockSpec(memory_space=pl.ANY)
    scalars = pl.BlockSpec(memory_space=pltpu.SMEM)
    dma = pltpu.SemaphoreType.DMA

    def run(*refs):
        kernel(chains, sectors, *refs)

    flops = 2 * 2 * width * slot * slot * (8 * slot + 6 * width)
    out = pl.pallas_call(
        run,
        out_shape=pltpu.VMEM((2, width, slot, slot), BF),
        in_specs=[anywhere] * 4 + [pl.BlockSpec(memory_space=pltpu.VMEM), scalars, scalars],
        out_specs=pl.BlockSpec(memory_space=pltpu.VMEM),
        scratch_shapes=[
            pltpu.VMEM((2, 3, width, slot, slot), BF),
            pltpu.VMEM((2, 4, slot, slot), BF),
            pltpu.VMEM((2, 4, slot, slot), BF),
            pltpu.VMEM((2, units, slot, 4 * UNIT_ROWS), BF),
            pltpu.VMEM((2, width * TILE, width * TILE), BF),
            pltpu.VMEM((2, width * TILE, width * TILE), BF),
            pltpu.VMEM((2, 2 * width * HALF, 2 * width * HALF), BF),
            pltpu.VMEM((4, width, UNIT_ROWS, slot), BF),
            pltpu.VMEM((width, 4, UNIT_ROWS, slot), BF),
            pltpu.VMEM((2, width, slot, slot), F32),
            dma((2,)),
            dma((2, steps)), dma((2, steps)),
            dma((2, steps)), dma((2, steps)),
            dma((2, steps)), dma((2, steps)),
            dma((4,)), dma((4,)),
            dma((2,)),
        ],
        compiler_params=pltpu.CompilerParams(
            collective_id=0, has_side_effects=True, vmem_limit_bytes=60 << 20
        ),
        cost_estimate=pl.CostEstimate(flops=flops, bytes_accessed=10 << 20, transcendentals=0),
    )(
        left_env[0, 0], right_env[0, 0], left_state[0, 0], right_state[0, 0],
        mpo, couple[0, :, 0], sizes,
    )
    left_out, right_out = pl.pallas_call(
        write_out,
        out_shape=[jax.ShapeDtypeStruct((width, slot, slot), BF)] * 2,
        in_specs=[pl.BlockSpec(memory_space=pltpu.VMEM)],
        out_specs=[anywhere] * 2,
        scratch_shapes=[dma((2, PARTS))],
        compiler_params=pltpu.CompilerParams(vmem_limit_bytes=16 << 20),
    )(out)
    return left_out[None, None], right_out[None, None]


def solution(mesh):
    blocks = P("chain", "sector", None, None, None)
    chains, sectors = mesh.shape["chain"], mesh.shape["sector"]

    def run(*args):
        return body(chains, sectors, *args)

    return jax.shard_map(
        run,
        mesh=mesh,
        in_specs=(blocks, blocks, blocks, blocks, P(), P("chain", None, "sector"), P()),
        out_specs=(blocks, blocks),
        check_vma=False,
    )
```

```python
import jax
import jax.numpy as jnp
from jax import lax
from jax.experimental import pallas as pl
from jax.experimental.pallas import tpu as pltpu
from jax.sharding import PartitionSpec as P

MESH = pl.DeviceIdType.MESH
BF = jnp.bfloat16
F32 = jnp.float32
OFFSETS = (0, 1, 1, 2)
STEP_ROWS = 32
UNIT_ROWS = STEP_ROWS
STATES = ((0,), (1, 2, 3))
TILE = 16
PARTS = 2
HALF = 8


def transposed_dot(a, b):
    return lax.dot_general(a, b, (((1,), (1,)), ((), ())), preferred_element_type=F32)


def kernel(
    chains, sectors,
    lenv, renv, lstate, rstate, mpo, couple, sizes,
    result,
    env, own, site, turned, mix0, mix3, mix12, inner, mixed, total,
    load_sem, x_send, x_recv, y_send, y_recv, d_send, d_recv, s_send, s_recv, edge_sem,
):
    width, slot = lenv.shape[0], lenv.shape[1]
    steps, units = slot // STEP_ROWS, slot // UNIT_ROWS
    i = lax.axis_index("chain")
    k = lax.axis_index("sector")
    core = lax.rem(k, 2)

    def at(chain_step, sector_step):
        return (
            lax.rem(i + chain_step + chains, chains),
            lax.rem(k + sector_step + sectors, sectors),
        )

    partner = (i, k + 1 - 2 * core)
    ahead, behind = at(1, 0), at(-1, 0)
    barrier = pltpu.get_barrier_semaphore()
    gets = (i > 0, i < chains - 1)
    gives = (gets[1], gets[0])

    def greet(*devices):
        for device in devices:
            pl.semaphore_signal(barrier, inc=1, device_id=device, device_id_type=MESH)

    greet(at(0, 2), at(0, -2), partner)

    @pl.when(gives[0])
    def _():
        greet(ahead, at(1, 1), at(1, 2))

    @pl.when(gives[1])
    def _():
        greet(behind, at(-1, -1), at(-1, -2))


    loads = [
        pltpu.make_async_copy(source, own.at[side], load_sem.at[side])
        for side, source in enumerate((lstate, rstate))
    ]
    for load in loads:
        load.start()
    ends = jnp.where(i == 0, 1, 0) + jnp.where(i == chains - 1, 1, 0)
    pl.semaphore_wait(barrier, 9 - 3 * ends)

    def rows(step):
        return pl.ds(pl.multiple_of(step * STEP_ROWS, STEP_ROWS), STEP_ROWS)

    def x_copy(side, step):
        return pltpu.make_async_remote_copy(
            (lenv, renv)[side].at[:, rows(step), :],
            env.at[side, 0, :, rows(step), :],
            x_send.at[side, step], x_recv.at[side, step],
            device_id=(ahead, behind)[side], device_id_type=MESH,
        )

    def y_copy(side, step):
        return pltpu.make_async_remote_copy(
            env.at[side, 0, :, rows(step), :],
            env.at[side, 2, :, rows(step), :],
            y_send.at[side, step], y_recv.at[side, step],
            device_id=(at(0, 2), at(0, -2))[side], device_id_type=MESH,
        )

    def d_copy(side, step):
        held = (2 * core, 2 * (1 - core))[side]
        return pltpu.make_async_remote_copy(
            env.at[side, held, :, rows(step), :],
            env.at[side, 1, :, rows(step), :],
            d_send.at[side, step], d_recv.at[side, step],
            device_id=partner, device_id_type=MESH,
        )

    def d_wait(side, step):
        pltpu.make_async_remote_copy(
            env.at[side, 0, :, rows(step), :],
            env.at[side, 1, :, rows(step), :],
            d_send.at[side, step], d_recv.at[side, step],
            device_id=partner, device_id_type=MESH,
        ).wait_recv()

    def s_copy(n):
        side, first, count, device = (
            (0, 0, 4, ahead), (1, 0, 1, behind), (1, 1, 2, at(-1, -1)), (1, 3, 1, at(-1, -2)),
        )[n]
        return pltpu.make_async_remote_copy(
            own.at[side, pl.ds(first, count)],
            site.at[side, pl.ds(first, count)],
            s_send.at[n], s_recv.at[n],
            device_id=device, device_id_type=MESH,
        )

    edges = ((0, lenv), (chains - 1, renv))

    def edge_copy(side):
        return pltpu.make_async_copy(edges[side][1], result.at[side], edge_sem.at[side])

    for side in range(2):
        @pl.when(gives[side])
        def _():
            x_copy(side, 0).start()

        @pl.when(i == edges[side][0])
        def _():
            edge_copy(side).start()

    for load in loads:
        load.wait()
    row_ids = lax.broadcasted_iota(jnp.int32, (slot, slot), 0)
    col_ids = lax.broadcasted_iota(jnp.int32, (slot, slot), 1)
    for s in range(4):
        source = k - OFFSETS[s]
        live = jnp.where(source >= 0, sizes[jnp.maximum(source, 0)], 0)
        live = jnp.where(couple[s] > 0, live, 0)
        keep = (row_ids < live) & (col_ids < sizes[k])
        own[0, s] = jnp.where(keep, own[0, s].astype(F32), 0.0).astype(BF)
        own[1, s] = jnp.where(keep, own[1, s].astype(F32), 0.0).T.astype(BF)
    for side in range(2):
        @pl.when(gives[side])
        def _():
            for n in STATES[side]:
                s_copy(n).start()

    def send(n, carry):
        for side in range(2):
            @pl.when(gives[side])
            def _():
                x_copy(side, n).start()
        return carry

    lax.fori_loop(1, steps, send, 0)

    def picker(count, member, tile):
        shape = (count * width * tile, width)
        r = lax.broadcasted_iota(jnp.int32, shape, 0)
        c = lax.broadcasted_iota(jnp.int32, shape, 1)
        return jnp.where(r // tile == c + member * width, 1.0, 0.0).astype(BF)

    def entries(s, t):
        r = lax.broadcasted_iota(jnp.int32, (width, width), 0)
        found = jnp.zeros((width, width), F32)
        for w in range(width):
            line = mpo[w, s].astype(F32)[t : t + 1, :]
            found = jnp.where(r == w, jnp.broadcast_to(line, (width, width)), found)
        return found.astype(BF)

    def spread(side, members, tile):
        count = len(members)
        picks = [picker(count, n, tile) for n in range(count)]
        full = jnp.zeros((count * width * tile, count * width * tile), F32)
        for n in range(count):
            part = jnp.zeros((count * width * tile, width), F32)
            for m in range(count):
                pair = (members[n], members[m]) if side == 0 else (members[m], members[n])
                part += jnp.dot(picks[m], entries(*pair), preferred_element_type=F32)
            part = part.astype(BF)
            full += transposed_dot(picks[n], part) if side == 0 else transposed_dot(part, picks[n])
        r = lax.broadcasted_iota(jnp.int32, full.shape, 0)
        c = lax.broadcasted_iota(jnp.int32, full.shape, 1)
        return jnp.where(lax.rem(r, tile) == lax.rem(c, tile), full, 0.0).astype(BF)

    for side in range(2):
        mix0[side] = spread(side, (0,), TILE)
        mix3[side] = spread(side, (3,), TILE)
        mix12[side] = spread(side, (1, 2), HALF)

    def clear(v, carry):
        for side in range(2):
            total[side, v] = jnp.zeros((slot, slot), F32)
        return carry

    lax.fori_loop(0, width, clear, 0)

    def turn():
        for side in range(2):
            @pl.when(gets[side])
            def _():
                for n in STATES[side]:
                    s_copy(n).wait_recv()
                for q in range(units):
                    part = site[side, :, q * UNIT_ROWS : (q + 1) * UNIT_ROWS, :]
                    turned[side, q] = part.reshape(4 * UNIT_ROWS, slot).astype(F32).T.astype(BF)

    def unit(side, q):
        span = pl.ds(pl.multiple_of(q * UNIT_ROWS, UNIT_ROWS), UNIT_ROWS)
        for s in range(4):
            held = env[side, (s + 1) // 2, :, span, :].reshape(width * UNIT_ROWS, slot)
            product = jnp.dot(held, site[side, s], preferred_element_type=F32)
            inner[s] = product.astype(BF).reshape(width, UNIT_ROWS, slot)
        for a in range(UNIT_ROWS // TILE):
            part = pl.ds(a * TILE, TILE)
            for s, weights in ((0, mix0), (3, mix3)):
                held = inner[s, :, part, :].reshape(width * TILE, slot)
                product = jnp.dot(weights[side], held, preferred_element_type=F32)
                mixed[:, s, part, :] = product.astype(BF).reshape(width, TILE, slot)
            held = inner[1:3, :, part, :].astype(F32)
            halves = []
            for h in range(2):
                some = held[:, :, h * HALF : (h + 1) * HALF, :].reshape(2 * width * HALF, slot)
                product = jnp.dot(mix12[side], some.astype(BF), preferred_element_type=F32)
                halves.append(product.reshape(2, width, HALF, slot))
            product = jnp.concatenate(halves, axis=2).astype(BF)
            mixed[:, 1, part, :] = product[0]
            mixed[:, 2, part, :] = product[1]
        for v in range(width):
            held = mixed[v].reshape(4 * UNIT_ROWS, slot)
            value = total[side, v] + jnp.dot(turned[side, q], held, preferred_element_type=F32)
            total[side, v] = value
            result[side, v] = value.astype(BF)

    def got(side):
        return jnp.where(side == 0, i, chains - 1 - i) > 0

    def step(c, carry):
        for side in range(2):
            @pl.when((c < steps) & gets[side])
            def _():
                x_copy(side, c).wait_recv()
                y_copy(side, c).start()

        @pl.when(c == 1)
        def _():
            turn()

        def one(side, carry):
            @pl.when(got(side) & (c >= 2))
            def _():
                d_wait(side, c - 2)
                unit(side, c - 2)

            @pl.when((c >= 1) & (c <= steps) & (side == 0))
            def _():
                for other in range(2):
                    @pl.when(gets[other])
                    def _():
                        y_copy(other, c - 1).wait_recv()
                        d_copy(other, c - 1).start()

            return carry

        lax.fori_loop(0, 2, one, 0)

        return carry

    lax.fori_loop(0, steps + 2, step, 0)

    def settle(c, carry):
        for side in range(2):
            @pl.when(gives[side])
            def _():
                x_copy(side, c).wait_send()

            @pl.when(gets[side])
            def _():
                y_copy(side, c).wait_send()
                d_copy(side, c).wait_send()
        return carry

    lax.fori_loop(0, steps, settle, 0)
    for side in range(2):
        @pl.when(gives[side])
        def _():
            for n in STATES[side]:
                s_copy(n).wait_send()

        @pl.when(i == edges[side][0])
        def _():
            edge_copy(side).wait()


def write_out(result, lout, rout, sems):
    size = lout.shape[0] // PARTS
    copies = [
        pltpu.make_async_copy(
            result.at[side, pl.ds(part * size, size)], target.at[pl.ds(part * size, size)], sems.at[side, part]
        )
        for part in range(PARTS)
        for side, target in enumerate((lout, rout))
    ]
    for copy in copies:
        copy.start()
    for copy in copies:
        copy.wait()


def body(chains, sectors, left_env, right_env, left_state, right_state, mpo, couple, sizes):
    width, slot = left_env.shape[2], left_env.shape[3]
    steps, units = slot // STEP_ROWS, slot // UNIT_ROWS
    anywhere = pl.BlockSpec(memory_space=pl.ANY)
    scalars = pl.BlockSpec(memory_space=pltpu.SMEM)
    dma = pltpu.SemaphoreType.DMA

    def run(*refs):
        kernel(chains, sectors, *refs)

    flops = 2 * 2 * width * slot * slot * (8 * slot + 6 * width)
    out = pl.pallas_call(
        run,
        out_shape=pltpu.VMEM((2, width, slot, slot), BF),
        in_specs=[anywhere] * 4 + [pl.BlockSpec(memory_space=pltpu.VMEM), scalars, scalars],
        out_specs=pl.BlockSpec(memory_space=pltpu.VMEM),
        scratch_shapes=[
            pltpu.VMEM((2, 3, width, slot, slot), BF),
            pltpu.VMEM((2, 4, slot, slot), BF),
            pltpu.VMEM((2, 4, slot, slot), BF),
            pltpu.VMEM((2, units, slot, 4 * UNIT_ROWS), BF),
            pltpu.VMEM((2, width * TILE, width * TILE), BF),
            pltpu.VMEM((2, width * TILE, width * TILE), BF),
            pltpu.VMEM((2, 2 * width * HALF, 2 * width * HALF), BF),
            pltpu.VMEM((4, width, UNIT_ROWS, slot), BF),
            pltpu.VMEM((width, 4, UNIT_ROWS, slot), BF),
            pltpu.VMEM((2, width, slot, slot), F32),
            dma((2,)),
            dma((2, steps)), dma((2, steps)),
            dma((2, steps)), dma((2, steps)),
            dma((2, steps)), dma((2, steps)),
            dma((4,)), dma((4,)),
            dma((2,)),
        ],
        compiler_params=pltpu.CompilerParams(
            collective_id=0, has_side_effects=True, vmem_limit_bytes=60 << 20
        ),
        cost_estimate=pl.CostEstimate(flops=flops, bytes_accessed=10 << 20, transcendentals=0),
    )(
        left_env[0, 0], right_env[0, 0], left_state[0, 0], right_state[0, 0],
        mpo, couple[0, :, 0], sizes,
    )
    left_out, right_out = pl.pallas_call(
        write_out,
        out_shape=[jax.ShapeDtypeStruct((width, slot, slot), BF)] * 2,
        in_specs=[pl.BlockSpec(memory_space=pltpu.VMEM)],
        out_specs=[anywhere] * 2,
        scratch_shapes=[dma((2, PARTS))],
        compiler_params=pltpu.CompilerParams(vmem_limit_bytes=16 << 20),
    )(out)
    return left_out[None, None], right_out[None, None]


def solution(mesh):
    blocks = P("chain", "sector", None, None, None)
    chains, sectors = mesh.shape["chain"], mesh.shape["sector"]

    def run(*args):
        return body(chains, sectors, *args)

    return jax.shard_map(
        run,
        mesh=mesh,
        in_specs=(blocks, blocks, blocks, blocks, P(), P("chain", None, "sector"), P()),
        out_specs=(blocks, blocks),
        check_vma=False,
    )
```

```python
import jax
import jax.numpy as jnp
from jax import lax
from jax.experimental import pallas as pl
from jax.experimental.pallas import tpu as pltpu
from jax.sharding import PartitionSpec as P

MESH = pl.DeviceIdType.MESH
BF = jnp.bfloat16
F32 = jnp.float32
OFFSETS = (0, 1, 1, 2)
STEP_ROWS = 32
UNIT_ROWS = STEP_ROWS
STATES = ((0,), (1, 2, 3))
TILE = 16
PARTS = 2
HALF = 8


def transposed_dot(a, b):
    return lax.dot_general(a, b, (((1,), (1,)), ((), ())), preferred_element_type=F32)


def kernel(
    chains, sectors,
    lenv, renv, lstate, rstate, mpo, couple, sizes,
    result,
    env, own, site, turned, mix0, mix3, mix12, inner, mixed, total,
    load_sem, x_send, x_recv, y_send, y_recv, d_send, d_recv, s_send, s_recv, edge_sem,
):
    width, slot = lenv.shape[0], lenv.shape[1]
    steps, units = slot // STEP_ROWS, slot // UNIT_ROWS
    i = lax.axis_index("chain")
    k = lax.axis_index("sector")
    core = lax.rem(k, 2)

    def at(chain_step, sector_step):
        return (
            lax.rem(i + chain_step + chains, chains),
            lax.rem(k + sector_step + sectors, sectors),
        )

    partner = (i, k + 1 - 2 * core)
    ahead, behind = at(1, 0), at(-1, 0)
    barrier = pltpu.get_barrier_semaphore()
    gets = (i > 0, i < chains - 1)
    gives = (gets[1], gets[0])

    def greet(*devices):
        for device in devices:
            pl.semaphore_signal(barrier, inc=1, device_id=device, device_id_type=MESH)

    greet(at(0, 2), at(0, -2), partner)

    @pl.when(gives[0])
    def _():
        greet(ahead, at(1, 1), at(1, 2))

    @pl.when(gives[1])
    def _():
        greet(behind, at(-1, -1), at(-1, -2))


    loads = [
        pltpu.make_async_copy(source, own.at[side], load_sem.at[side])
        for side, source in enumerate((lstate, rstate))
    ]
    for load in loads:
        load.start()
    ends = jnp.where(i == 0, 1, 0) + jnp.where(i == chains - 1, 1, 0)
    pl.semaphore_wait(barrier, 9 - 3 * ends)

    def rows(step):
        return pl.ds(pl.multiple_of(step * STEP_ROWS, STEP_ROWS), STEP_ROWS)

    def x_copy(side, step):
        return pltpu.make_async_remote_copy(
            (lenv, renv)[side].at[:, rows(step), :],
            env.at[side, 0, :, rows(step), :],
            x_send.at[side, step], x_recv.at[side, step],
            device_id=(ahead, behind)[side], device_id_type=MESH,
        )

    def y_copy(side, step):
        return pltpu.make_async_remote_copy(
            env.at[side, 0, :, rows(step), :],
            env.at[side, 2, :, rows(step), :],
            y_send.at[side, step], y_recv.at[side, step],
            device_id=(at(0, 2), at(0, -2))[side], device_id_type=MESH,
        )

    def d_copy(side, step):
        held = (2 * core, 2 * (1 - core))[side]
        return pltpu.make_async_remote_copy(
            env.at[side, held, :, rows(step), :],
            env.at[side, 1, :, rows(step), :],
            d_send.at[side, step], d_recv.at[side, step],
            device_id=partner, device_id_type=MESH,
        )

    def d_wait(side, step):
        pltpu.make_async_remote_copy(
            env.at[side, 0, :, rows(step), :],
            env.at[side, 1, :, rows(step), :],
            d_send.at[side, step], d_recv.at[side, step],
            device_id=partner, device_id_type=MESH,
        ).wait_recv()

    def s_copy(n):
        side, first, count, device = (
            (0, 0, 4, ahead), (1, 0, 1, behind), (1, 1, 2, at(-1, -1)), (1, 3, 1, at(-1, -2)),
        )[n]
        return pltpu.make_async_remote_copy(
            own.at[side, pl.ds(first, count)],
            site.at[side, pl.ds(first, count)],
            s_send.at[n], s_recv.at[n],
            device_id=device, device_id_type=MESH,
        )

    edges = ((0, lenv), (chains - 1, renv))

    def edge_copy(side):
        return pltpu.make_async_copy(edges[side][1], result.at[side], edge_sem.at[side])

    for side in range(2):
        @pl.when(gives[side])
        def _():
            x_copy(side, 0).start()

        @pl.when(i == edges[side][0])
        def _():
            edge_copy(side).start()

    for load in loads:
        load.wait()
    row_ids = lax.broadcasted_iota(jnp.int32, (slot, slot), 0)
    col_ids = lax.broadcasted_iota(jnp.int32, (slot, slot), 1)
    for s in range(4):
        source = k - OFFSETS[s]
        live = jnp.where(source >= 0, sizes[jnp.maximum(source, 0)], 0)
        live = jnp.where(couple[s] > 0, live, 0)
        keep = (row_ids < live) & (col_ids < sizes[k])
        own[0, s] = jnp.where(keep, own[0, s].astype(F32), 0.0).astype(BF)
        own[1, s] = jnp.where(keep, own[1, s].astype(F32), 0.0).T.astype(BF)
    for side in range(2):
        @pl.when(gives[side])
        def _():
            for n in STATES[side]:
                s_copy(n).start()

    def send(n, carry):
        for side in range(2):
            @pl.when(gives[side])
            def _():
                x_copy(side, n).start()
        return carry

    lax.fori_loop(1, steps, send, 0)

    def picker(count, member, tile):
        shape = (count * width * tile, width)
        r = lax.broadcasted_iota(jnp.int32, shape, 0)
        c = lax.broadcasted_iota(jnp.int32, shape, 1)
        return jnp.where(r // tile == c + member * width, 1.0, 0.0).astype(BF)

    def entries(s, t):
        r = lax.broadcasted_iota(jnp.int32, (width, width), 0)
        found = jnp.zeros((width, width), F32)
        for w in range(width):
            line = mpo[w, s].astype(F32)[t : t + 1, :]
            found = jnp.where(r == w, jnp.broadcast_to(line, (width, width)), found)
        return found.astype(BF)

    def spread(side, members, tile):
        count = len(members)
        picks = [picker(count, n, tile) for n in range(count)]
        full = jnp.zeros((count * width * tile, count * width * tile), F32)
        for n in range(count):
            part = jnp.zeros((count * width * tile, width), F32)
            for m in range(count):
                pair = (members[n], members[m]) if side == 0 else (members[m], members[n])
                part += jnp.dot(picks[m], entries(*pair), preferred_element_type=F32)
            part = part.astype(BF)
            full += transposed_dot(picks[n], part) if side == 0 else transposed_dot(part, picks[n])
        r = lax.broadcasted_iota(jnp.int32, full.shape, 0)
        c = lax.broadcasted_iota(jnp.int32, full.shape, 1)
        return jnp.where(lax.rem(r, tile) == lax.rem(c, tile), full, 0.0).astype(BF)

    for side in range(2):
        mix0[side] = spread(side, (0,), TILE)
        mix3[side] = spread(side, (3,), TILE)
        mix12[side] = spread(side, (1, 2), HALF)

    def clear(v, carry):
        for side in range(2):
            total[side, v] = jnp.zeros((slot, slot), F32)
        return carry

    lax.fori_loop(0, width, clear, 0)

    def turn():
        for side in range(2):
            @pl.when(gets[side])
            def _():
                for n in STATES[side]:
                    s_copy(n).wait_recv()
                for q in range(units):
                    part = site[side, :, q * UNIT_ROWS : (q + 1) * UNIT_ROWS, :]
                    turned[side, q] = part.reshape(4 * UNIT_ROWS, slot).astype(F32).T.astype(BF)

    def unit(side, q, final):
        span = pl.ds(pl.multiple_of(q * UNIT_ROWS, UNIT_ROWS), UNIT_ROWS)
        for s in range(4):
            held = env[side, (s + 1) // 2, :, span, :].reshape(width * UNIT_ROWS, slot)
            product = jnp.dot(held, site[side, s], preferred_element_type=F32)
            inner[s] = product.astype(BF).reshape(width, UNIT_ROWS, slot)
        for a in range(UNIT_ROWS // TILE):
            part = pl.ds(a * TILE, TILE)
            for s, weights in ((0, mix0), (3, mix3)):
                held = inner[s, :, part, :].reshape(width * TILE, slot)
                product = jnp.dot(weights[side], held, preferred_element_type=F32)
                mixed[:, s, part, :] = product.astype(BF).reshape(width, TILE, slot)
            held = inner[1:3, :, part, :].astype(F32)
            halves = []
            for h in range(2):
                some = held[:, :, h * HALF : (h + 1) * HALF, :].reshape(2 * width * HALF, slot)
                product = jnp.dot(mix12[side], some.astype(BF), preferred_element_type=F32)
                halves.append(product.reshape(2, width, HALF, slot))
            product = jnp.concatenate(halves, axis=2).astype(BF)
            mixed[:, 1, part, :] = product[0]
            mixed[:, 2, part, :] = product[1]
        for v in range(width):
            held = mixed[v].reshape(4 * UNIT_ROWS, slot)
            value = total[side, v] + jnp.dot(turned[side, q], held, preferred_element_type=F32)
            if final:
                result[side, v] = value.astype(BF)
            else:
                total[side, v] = value

    def got(side):
        return jnp.where(side == 0, i, chains - 1 - i) > 0

    def step(c, carry):
        for side in range(2):
            @pl.when((c < steps) & gets[side])
            def _():
                x_copy(side, c).wait_recv()
                y_copy(side, c).start()

        @pl.when(c == 1)
        def _():
            turn()

        def one(side, carry):
            @pl.when(got(side) & (c >= 2))
            def _():
                d_wait(side, c - 2)
                unit(side, c - 2, False)

            @pl.when((c >= 1) & (c <= steps) & (side == 0))
            def _():
                for other in range(2):
                    @pl.when(gets[other])
                    def _():
                        y_copy(other, c - 1).wait_recv()
                        d_copy(other, c - 1).start()

            return carry

        lax.fori_loop(0, 2, one, 0)

        return carry

    lax.fori_loop(0, steps + 1, step, 0)

    def finish(side, carry):
        @pl.when(got(side))
        def _():
            d_wait(side, steps - 1)
            unit(side, units - 1, True)

        return carry

    lax.fori_loop(0, 2, finish, 0)

    def settle(c, carry):
        for side in range(2):
            @pl.when(gives[side])
            def _():
                x_copy(side, c).wait_send()

            @pl.when(gets[side])
            def _():
                y_copy(side, c).wait_send()
                d_copy(side, c).wait_send()
        return carry

    lax.fori_loop(0, steps, settle, 0)
    for side in range(2):
        @pl.when(gives[side])
        def _():
            for n in STATES[side]:
                s_copy(n).wait_send()

        @pl.when(i == edges[side][0])
        def _():
            edge_copy(side).wait()


def write_out(result, lout, rout, sems):
    size = lout.shape[0] // PARTS
    copies = [
        pltpu.make_async_copy(
            result.at[side, pl.ds(part * size, size)], target.at[pl.ds(part * size, size)], sems.at[side, part]
        )
        for part in range(PARTS)
        for side, target in enumerate((lout, rout))
    ]
    for copy in copies:
        copy.start()
    for copy in copies:
        copy.wait()


def body(chains, sectors, left_env, right_env, left_state, right_state, mpo, couple, sizes):
    width, slot = left_env.shape[2], left_env.shape[3]
    steps, units = slot // STEP_ROWS, slot // UNIT_ROWS
    anywhere = pl.BlockSpec(memory_space=pl.ANY)
    scalars = pl.BlockSpec(memory_space=pltpu.SMEM)
    dma = pltpu.SemaphoreType.DMA

    def run(*refs):
        kernel(chains, sectors, *refs)

    flops = 2 * 2 * width * slot * slot * (8 * slot + 6 * width)
    out = pl.pallas_call(
        run,
        out_shape=pltpu.VMEM((2, width, slot, slot), BF),
        in_specs=[anywhere] * 4 + [pl.BlockSpec(memory_space=pltpu.VMEM), scalars, scalars],
        out_specs=pl.BlockSpec(memory_space=pltpu.VMEM),
        scratch_shapes=[
            pltpu.VMEM((2, 3, width, slot, slot), BF),
            pltpu.VMEM((2, 4, slot, slot), BF),
            pltpu.VMEM((2, 4, slot, slot), BF),
            pltpu.VMEM((2, units, slot, 4 * UNIT_ROWS), BF),
            pltpu.VMEM((2, width * TILE, width * TILE), BF),
            pltpu.VMEM((2, width * TILE, width * TILE), BF),
            pltpu.VMEM((2, 2 * width * HALF, 2 * width * HALF), BF),
            pltpu.VMEM((4, width, UNIT_ROWS, slot), BF),
            pltpu.VMEM((width, 4, UNIT_ROWS, slot), BF),
            pltpu.VMEM((2, width, slot, slot), F32),
            dma((2,)),
            dma((2, steps)), dma((2, steps)),
            dma((2, steps)), dma((2, steps)),
            dma((2, steps)), dma((2, steps)),
            dma((4,)), dma((4,)),
            dma((2,)),
        ],
        compiler_params=pltpu.CompilerParams(
            collective_id=0, has_side_effects=True, vmem_limit_bytes=60 << 20
        ),
        cost_estimate=pl.CostEstimate(flops=flops, bytes_accessed=10 << 20, transcendentals=0),
    )(
        left_env[0, 0], right_env[0, 0], left_state[0, 0], right_state[0, 0],
        mpo, couple[0, :, 0], sizes,
    )
    left_out, right_out = pl.pallas_call(
        write_out,
        out_shape=[jax.ShapeDtypeStruct((width, slot, slot), BF)] * 2,
        in_specs=[pl.BlockSpec(memory_space=pltpu.VMEM)],
        out_specs=[anywhere] * 2,
        scratch_shapes=[dma((2, PARTS))],
        compiler_params=pltpu.CompilerParams(vmem_limit_bytes=16 << 20),
    )(out)
    return left_out[None, None], right_out[None, None]


def solution(mesh):
    blocks = P("chain", "sector", None, None, None)
    chains, sectors = mesh.shape["chain"], mesh.shape["sector"]

    def run(*args):
        return body(chains, sectors, *args)

    return jax.shard_map(
        run,
        mesh=mesh,
        in_specs=(blocks, blocks, blocks, blocks, P(), P("chain", None, "sector"), P()),
        out_specs=(blocks, blocks),
        check_vma=False,
    )
```
